32 devices in a mesh: pipe: 2 (over y), ctx: 4 (over x, core), tp: 4 (over z).
Axes of the slice: x: 2, y: 2, z: 4, core: 2. Of those that a mesh axis runs over, the one named last changes fastest.
Arguments:
- x_in: bfloat16 [2, 512, 8192], P(None, 'ctx', 'tp'), may hold values from -6 to 6
- hidden_in: bfloat16 [2, 512, 8192], P(None, ('ctx', 'tp')), may hold values from -6 to 6
- gate_z: bfloat16 [2, 2, 512, 8192], P('pipe', None, 'ctx', 'tp'), may hold values from -6 to 6
- out_proj: bfloat16 [8192, 8192], P('tp', 'ctx'), may hold values from -0.0625 to 0.0625
- in_proj: bfloat16 [8192, 8192], P('tp', 'ctx'), may hold values from -0.0625 to 0.0625
- norm_gain: float32 [8192], replicated, may hold values from 0.1 to 1.9
- conv_weight: float32 [2, 4, 8192], P('pipe', None, 'tp'), may hold values from -3 to 3
- conv_bias: float32 [2, 8192], P('pipe', 'tp'), may hold values from -3 to 3
- x_proj: bfloat16 [2, 8192, 544], P('pipe', 'tp'), may hold values from -0.0625 to 0.0625
- dt_proj: bfloat16 [2, 512, 8192], P('pipe', None, 'tp'), may hold values from -0.25 to 0.25
- dt_bias: float32 [2, 8192], P('pipe', 'tp'), may hold values from -3 to -1
- decay_rate: float32 [2, 16, 8192], P('pipe', None, 'tp'), may hold values from 0.001953125 to 1
- skip: float32 [2, 8192], P('pipe', 'tp'), may hold values from 0.1 to 1.9
Outputs:
- mixed: bfloat16 [2, 2, 512, 8192], P('pipe', None, 'ctx', 'tp')
The draws below stay inside these ranges and needn't reach their ends.
All inputs are finite; a program needn't handle non-finite values.
Results may differ from the reference program's by a relative error of at most 0.017.
Values may be sent and summed in bfloat16 or wider, within the bound.
A program may use at most 128 MiB of HBM per device.

```python
import math
import jax
import jax.numpy as jnp
from jax import lax

D = 8192
INNER = 8192
NSTATE = 16
RANK = 512
CONVW = 4
MICRO = 2
SECTIONS = 2
TOKENS = 512


def steps_of(own_key, extent, pieces, least, top_value):
    loudness, own = 1.0, jax.random.fold_in(own_key, 6)
    for dim, blocks in pieces:
        heights = jnp.exp(jax.random.uniform(jax.random.fold_in(own, dim), (blocks,), jnp.float32, least / len(pieces), top_value / len(pieces)))
        loudness = loudness * jnp.repeat(heights, extent[dim] // blocks).reshape([-1 if axis == dim else 1 for axis in range(len(extent))])
    return loudness


def normal_values(own_key, shape, width, bound, split=(), held_as=jnp.bfloat16):
    gain = steps_of(own_key, shape, split, -0.22, 0.18) if split else 1.0
    values = jax.random.normal(own_key, shape, jnp.float32) * width * gain
    return jnp.minimum(jnp.maximum(values, -bound), bound).astype(held_as)


def setup_inputs(seed: int = 0) -> dict:
    key_list = jax.random.split(jax.random.key(seed), 14)
    x_in = normal_values(key_list[0], (MICRO, TOKENS, INNER), 1.0, 6.0, ((1, 4), (2, 4)))
    hidden_in = normal_values(key_list[1], (MICRO, TOKENS, D), 1.0, 6.0, ((1, 16),))
    gate_z = normal_values(key_list[2], (SECTIONS, MICRO, TOKENS, INNER), 1.0, 6.0, ((0, 2), (2, 4), (3, 4)))
    out_proj = normal_values(key_list[3], (INNER, D), INNER ** -0.5, 0.0625, ((0, 4), (1, 4)))
    in_proj = normal_values(key_list[4], (INNER, D), D ** -0.5, 0.0625, ((0, 4), (1, 4)))
    norm_gain = jnp.clip(1.0 + 0.18 * jax.random.normal(key_list[5], (D,), jnp.float32), 0.1, 1.9)
    conv_weight = normal_values(key_list[6], (SECTIONS, CONVW, INNER), CONVW ** -0.5, 3.0, ((0, 2), (2, 4)), jnp.float32)
    conv_bias = normal_values(key_list[7], (SECTIONS, INNER), 0.5, 3.0, ((0, 2), (1, 4)), jnp.float32)
    x_proj = normal_values(key_list[8], (SECTIONS, INNER, RANK + 2 * NSTATE), INNER ** -0.5, 0.0625, ((0, 2), (1, 4)))
    dt_proj = normal_values(key_list[9], (SECTIONS, RANK, INNER), RANK ** -0.5, 0.25, ((0, 2), (2, 4)))
    dt_bias = jnp.clip(-3.0 + 2.0 * jax.random.uniform(key_list[10], (SECTIONS, INNER), jnp.float32) ** steps_of(key_list[10], (SECTIONS, INNER), ((0, 2), (1, 4)), -0.2, 0.2), -3.0, -1.0)
    decay_rate = jnp.clip(jnp.exp(math.log(1.0) - 6.2383246 * jax.random.uniform(key_list[11], (SECTIONS, NSTATE, INNER), jnp.float32) ** steps_of(key_list[11], (SECTIONS, NSTATE, INNER), ((0, 2), (2, 4)), -0.2, 0.2)), 0.001953125, 1.0)
    skip = jnp.clip(1.0 + 0.18 * jax.random.normal(key_list[12], (SECTIONS, INNER), jnp.float32), 0.1, 1.9)
    return dict(x_in=x_in, hidden_in=hidden_in, gate_z=gate_z, out_proj=out_proj, in_proj=in_proj, norm_gain=norm_gain, conv_weight=conv_weight, conv_bias=conv_bias, x_proj=x_proj, dt_proj=dt_proj, dt_bias=dt_bias, decay_rate=decay_rate, skip=skip)


def run_section(inputs, gate, taps, bias, proj_weight, rate_weight, rate_bias, decay, skip_coef):
    count = inputs.shape[0]
    wide_in = inputs.astype(jnp.float32)
    padded = jnp.concatenate([jnp.zeros((CONVW - 1, INNER), jnp.float32), wide_in], axis=0)
    convolved = bias[None, :] + jnp.zeros((count, INNER), jnp.float32)
    for offset in range(CONVW):
        convolved = convolved + taps[offset][None, :] * padded[offset:offset + count]
    activated = jax.nn.silu(convolved).astype(jnp.bfloat16)
    projected = jnp.dot(activated, proj_weight, preferred_element_type=jnp.float32)
    rate_low = projected[:, :RANK]
    rate_normed = (rate_low * lax.rsqrt(lax.optimization_barrier(jnp.mean(rate_low * rate_low, axis=1, keepdims=True)) + 1e-06)).astype(jnp.bfloat16)
    step_size = jax.nn.softplus(jnp.dot(rate_normed, rate_weight, preferred_element_type=jnp.float32) + rate_bias[None, :])
    input_map = projected[:, RANK:RANK + NSTATE]
    output_map = projected[:, RANK + NSTATE:]
    active_wide = activated.astype(jnp.float32)

    def advance(state, row):
        step_row, act_row, in_row, out_row = row
        state = jnp.exp(-step_row[None, :] * decay) * state + in_row[:, None] * (step_row * act_row)[None, :]
        return (state, lax.optimization_barrier(jnp.sum(out_row[:, None] * state, axis=0)))
    start_state = jnp.zeros((NSTATE, INNER), jnp.float32)
    _, response = lax.scan(advance, start_state, (step_size, active_wide, input_map, output_map))
    response = response + skip_coef[None, :] * active_wide
    return (response * jax.nn.silu(gate.astype(jnp.float32))).astype(jnp.bfloat16)

def reference(x_in, hidden_in, gate_z, out_proj, in_proj, norm_gain, conv_weight, conv_bias, x_proj, dt_proj, dt_bias, decay_rate, skip):
    first_out = []
    second_out = []
    for batch in range(MICRO):
        mixed_first = run_section(x_in[batch], gate_z[0, batch], conv_weight[0], conv_bias[0], x_proj[0], dt_proj[0], dt_bias[0], decay_rate[0], skip[0])
        link = jnp.dot(mixed_first, out_proj, preferred_element_type=jnp.float32)
        carried = (hidden_in[batch].astype(jnp.float32) + link).astype(jnp.bfloat16)
        carried = lax.optimization_barrier(carried)
        wide = carried.astype(jnp.float32)
        normed = (wide * lax.rsqrt(lax.optimization_barrier(jnp.mean(wide * wide, axis=1, keepdims=True)) + 1e-05) * norm_gain[None, :]).astype(jnp.bfloat16)
        inputs = jnp.dot(normed, in_proj.T, preferred_element_type=jnp.float32).astype(jnp.bfloat16)
        mixed_second = run_section(inputs, gate_z[1, batch], conv_weight[1], conv_bias[1], x_proj[1], dt_proj[1], dt_bias[1], decay_rate[1], skip[1])
        first_out.append(mixed_first)
        second_out.append(mixed_second)
    return jnp.stack([jnp.stack(first_out, axis=0), jnp.stack(second_out, axis=0)], axis=0)
```

```python
import functools

import jax
import jax.numpy as jnp
from jax import lax
from jax.experimental import pallas as pl
from jax.experimental.pallas import tpu as pltpu
from jax.sharding import PartitionSpec as P

LANES = 128
TILE = 1024
ROWS = 8
LOG2E = 1.4426950408889634
BF16 = jnp.bfloat16
F32 = jnp.float32


def params():
    return pltpu.CompilerParams(vmem_limit_bytes=32 * 1024 * 1024)


def rotated(block, axis, distance):
    count = lax.axis_size(axis)
    return lax.ppermute(block, axis, [(i, (i + distance) % count) for i in range(count)])


def shifted(block, axis, distance):
    count = lax.axis_size(axis)
    return lax.ppermute(block, axis, [(i - distance, i) for i in range(distance, count)])


def swapped(block):
    return lax.ppermute(block, "pipe", [(0, 1), (1, 0)])


def sibling(block):
    count = lax.axis_size("ctx")
    return lax.ppermute(block, "ctx", [(i, i ^ 1) for i in range(count)])


def swap_shared(weight):
    half = weight.shape[0] // 2
    core = lax.axis_index("ctx") % 2
    part = swapped(lax.dynamic_slice_in_dim(weight, core * half, half, 0))
    rest = sibling(part)
    first = core == 0
    return jnp.concatenate([jnp.where(first, part, rest), jnp.where(first, rest, part)], axis=0)


def conv_kernel(x_ref, rim_ref, w_ref, b_ref, proj_ref, act_ref, part_ref, pad, total):
    count, width = x_ref.shape
    taps = w_ref.shape[0]
    rim = rim_ref.shape[0]
    pad[:rim, :] = rim_ref[...].astype(F32)
    pad[rim:, :] = x_ref[...].astype(F32)
    for row in range(0, count, 32):
        value = b_ref[...] + jnp.zeros((32, width), F32)
        for k in range(taps):
            start = rim - (taps - 1) + row + k
            value = value + w_ref[k : k + 1, :] * pad[start : start + 32, :]
        act_ref[row : row + 32, :] = (value / (1.0 + jnp.exp(-value))).astype(BF16)
    product = jnp.dot(act_ref[...], proj_ref[...], preferred_element_type=F32)
    step = pl.program_id(0)

    @pl.when(step == 0)
    def _():
        total[...] = product

    @pl.when(step > 0)
    def _():
        total[...] += product

    @pl.when(step == pl.num_programs(0) - 1)
    def _():
        part_ref[...] = total[...].astype(BF16)


def conv_project(inputs, rim, conv_weight, conv_bias, x_proj):
    count, width = inputs.shape
    cols = x_proj.shape[1]
    block = 512
    return pl.pallas_call(
        conv_kernel,
        grid=(width // block,),
        in_specs=[
            pl.BlockSpec((count, block), lambda c: (0, c)),
            pl.BlockSpec((rim.shape[0], block), lambda c: (0, c)),
            pl.BlockSpec((conv_weight.shape[0], block), lambda c: (0, c)),
            pl.BlockSpec((1, block), lambda c: (0, c)),
            pl.BlockSpec((block, cols), lambda c: (c, 0)),
        ],
        out_specs=[
            pl.BlockSpec((count, block), lambda c: (0, c)),
            pl.BlockSpec((count, cols), lambda c: (0, 0)),
        ],
        out_shape=[
            jax.ShapeDtypeStruct((count, width), BF16),
            jax.ShapeDtypeStruct((count, cols), BF16),
        ],
        scratch_shapes=[
            pltpu.VMEM((count + rim.shape[0], block), F32),
            pltpu.VMEM((count, cols), F32),
        ],
        compiler_params=params(),
        name="conv_project",
    )(inputs, rim, conv_weight, conv_bias, x_proj)


def scan_kernel(nstate, maps_ref, rate_ref, dt_ref, bias_ref, act_ref, decay_ref,
                resp_ref, cum_ref, end_ref, steps, driven, wide):
    count = rate_ref.shape[0]
    wide[...] = jnp.dot(rate_ref[...], dt_ref[...], preferred_element_type=F32)

    def spread(group, carry):
        base = pl.multiple_of(group * 16, 16)
        for j in range(ROWS):
            lanes = slice(j * LANES, (j + 1) * LANES)
            raw = wide[pl.ds(base, 16), lanes] + bias_ref[:, lanes]
            rate = jnp.maximum(raw, 0.0) + jnp.log1p(jnp.exp(-jnp.abs(raw)))
            active = act_ref[pl.ds(base, 16), lanes].astype(F32)
            steps[pl.ds(base * ROWS + j, 16, stride=ROWS), :] = rate
            driven[pl.ds(base * ROWS + j, 16, stride=ROWS), :] = rate * active
        return carry

    lax.fori_loop(0, count // 16, spread, 0)

    def one(t, carry):
        state, cum = carry
        rows = pl.ds(pl.multiple_of(t * ROWS, ROWS), ROWS)
        rate = steps[rows, :]
        drive = driven[rows, :]
        later, sums = [], [None] * 4
        for n in range(nstate):
            h = jnp.exp2(rate * decay_ref[n]) * state[n] + maps_ref[t, n] * drive
            later.append(h)
            term = maps_ref[t, nstate + n] * h
            sums[n % 4] = term if sums[n % 4] is None else sums[n % 4] + term
        cum = cum + rate
        resp_ref[rows, :] = (sums[0] + sums[1]) + (sums[2] + sums[3])
        cum_ref[rows, :] = cum
        return tuple(later), cum

    def pair(g, carry):
        return one(2 * g + 1, one(2 * g, carry))

    zero = jnp.zeros((ROWS, LANES), F32)
    state, cum = lax.fori_loop(0, count // 2, pair, ((zero,) * nstate, zero))
    for n in range(nstate):
        end_ref[n] = state[n]
    end_ref[nstate] = cum


def local_scan(maps, rate_normed, dt_proj, dt_bias, activated, decay):
    count, width = activated.shape
    rank = dt_proj.shape[0]
    nstate = decay.shape[0]
    tiles = width // TILE
    rows = pl.BlockSpec((None, count * ROWS, LANES), lambda c: (c, 0, 0))
    return pl.pallas_call(
        functools.partial(scan_kernel, nstate),
        grid=(tiles,),
        in_specs=[
            pl.BlockSpec(memory_space=pltpu.SMEM),
            pl.BlockSpec((count, rank), lambda c: (0, 0)),
            pl.BlockSpec((rank, TILE), lambda c: (0, c)),
            pl.BlockSpec((1, TILE), lambda c: (0, c)),
            pl.BlockSpec((count, TILE), lambda c: (0, c)),
            pl.BlockSpec((nstate, ROWS, LANES), lambda c: (0, c, 0)),
        ],
        out_specs=[rows, rows, pl.BlockSpec((nstate + 1, ROWS, LANES), lambda c: (0, c, 0))],
        out_shape=[
            jax.ShapeDtypeStruct((tiles, count * ROWS, LANES), F32),
            jax.ShapeDtypeStruct((tiles, count * ROWS, LANES), F32),
            jax.ShapeDtypeStruct((nstate + 1, tiles * ROWS, LANES), F32),
        ],
        scratch_shapes=[
            pltpu.VMEM((count * ROWS, LANES), F32),
            pltpu.VMEM((count * ROWS, LANES), F32),
            pltpu.VMEM((count, TILE), F32),
        ],
        compiler_params=params(),
        name="local_scan",
    )(maps, rate_normed, dt_proj, dt_bias, activated, decay)


def finish_kernel(nstate, earlier, maps_ref, resp_ref, cum_ref, decay_ref, skip_ref,
                  act_ref, gate_ref, *rest):
    ends, out_ref, total, enter = rest[:earlier], rest[earlier], rest[earlier + 1], rest[earlier + 2]
    count = act_ref.shape[0]
    for n in range(nstate):
        value, passed = ends[0][n], ends[0][nstate]
        for block in ends[1:]:
            value = value + jnp.exp2(decay_ref[n] * passed) * block[n]
            passed = passed + block[nstate]
        enter[n] = value

    def one(t):
        rows = pl.ds(pl.multiple_of(t * ROWS, ROWS), ROWS)
        cum = cum_ref[rows, :]
        sums = [resp_ref[rows, :], None, None, None]
        for n in range(nstate):
            term = maps_ref[t, nstate + n] * (jnp.exp2(cum * decay_ref[n]) * enter[n])
            sums[n % 4] = term if sums[n % 4] is None else sums[n % 4] + term
        total[rows, :] = (sums[0] + sums[1]) + (sums[2] + sums[3])

    def pair(g, carry):
        one(2 * g)
        one(2 * g + 1)
        return carry

    lax.fori_loop(0, count // 2, pair, 0)

    def gather(group, carry):
        base = pl.multiple_of(group * 16, 16)
        for j in range(ROWS):
            lanes = slice(j * LANES, (j + 1) * LANES)
            active = act_ref[pl.ds(base, 16), lanes].astype(F32)
            gate = gate_ref[pl.ds(base, 16), lanes].astype(F32)
            value = total[pl.ds(base * ROWS + j, 16, stride=ROWS), :] + skip_ref[:, lanes] * active
            out_ref[pl.ds(base, 16), lanes] = (value * (gate / (1.0 + jnp.exp(-gate)))).astype(BF16)
        return carry

    lax.fori_loop(0, count // 16, gather, 0)


def finish(maps, response, cum, decay, skip, activated, gate, ends):
    count, width = activated.shape
    nstate = decay.shape[0]
    rows = pl.BlockSpec((None, count * ROWS, LANES), lambda c: (c, 0, 0))
    flat = pl.BlockSpec((count, TILE), lambda c: (0, c))
    return pl.pallas_call(
        functools.partial(finish_kernel, nstate, len(ends)),
        grid=(width // TILE,),
        in_specs=[
            pl.BlockSpec(memory_space=pltpu.SMEM),
            rows,
            rows,
            pl.BlockSpec((nstate, ROWS, LANES), lambda c: (0, c, 0)),
            pl.BlockSpec((1, TILE), lambda c: (0, c)),
            flat,
            flat,
        ]
        + [pl.BlockSpec((nstate + 1, ROWS, LANES), lambda c: (0, c, 0))] * len(ends),
        out_specs=flat,
        out_shape=jax.ShapeDtypeStruct((count, width), BF16),
        scratch_shapes=[
            pltpu.VMEM((count * ROWS, LANES), F32),
            pltpu.VMEM((nstate, ROWS, LANES), F32),
        ],
        compiler_params=params(),
        name="finish_mixer",
    )(maps, response, cum, decay, skip, activated, gate, *ends)


def mixer(inputs, gate, small, x_proj, dt_proj):
    conv_weight, conv_bias, dt_bias, decay, skip = small
    rank = dt_proj.shape[0]
    nstate = decay.shape[0]
    rim = shifted(inputs[-16:], "ctx", 1)
    activated, partial = conv_project(inputs, rim, conv_weight, conv_bias, x_proj)
    parts = [partial] + [rotated(partial, "tp", s) for s in range(1, lax.axis_size("tp"))]
    projected = parts[0].astype(F32)
    for part in parts[1:]:
        projected = projected + part.astype(F32)
    low = projected[:, :rank]
    rate_normed = (
        low * lax.rsqrt(jnp.mean(low * low, axis=1, keepdims=True) + 1e-06)
    ).astype(BF16)
    maps = projected[:, rank:]
    decay_tiles = (decay * -LOG2E).reshape(nstate, -1, LANES)
    response, cum, end = local_scan(maps, rate_normed, dt_proj, dt_bias, activated, decay_tiles)
    ends = [shifted(end, "ctx", s) for s in range(1, lax.axis_size("ctx"))]
    return finish(maps, response, cum, decay_tiles, skip, activated, gate, ends)


def shards(
    x_in,
    hidden_in,
    gate_z,
    out_proj,
    in_proj,
    norm_gain,
    conv_weight,
    conv_bias,
    x_proj,
    dt_proj,
    dt_bias,
    decay_rate,
    skip,
):
    segment = lax.axis_index("pipe")
    first = segment == 0
    ctx, tp = lax.axis_size("ctx"), lax.axis_size("tp")
    place, column = lax.axis_index("ctx"), lax.axis_index("tp")
    block = hidden_in.shape[1]
    depth = out_proj.shape[1]
    width = x_in.shape[2]

    own_small = jnp.concatenate(
        [conv_weight[0], conv_bias, dt_bias, decay_rate[0], skip], axis=0
    )
    other_small = swapped(own_small)
    other_x = swap_shared(x_proj[0])
    held_dt, other_x = lax.optimization_barrier((dt_proj[0], other_x))
    other_dt = swap_shared(held_dt)
    own_gate = lax.dynamic_index_in_dim(gate_z[0], segment, 0, False)
    held_gate, other_dt = lax.optimization_barrier(
        (lax.dynamic_index_in_dim(gate_z[0], 1 - segment, 0, False), other_dt)
    )
    other_gate = swapped(held_gate)
    taps = conv_weight.shape[1]
    nstate = decay_rate.shape[1]

    def weights(section):
        mine = first if section == 0 else jnp.logical_not(first)
        small = jnp.where(mine, own_small, other_small)
        parts = (
            small[:taps],
            small[taps : taps + 1],
            small[taps + 1 : taps + 2],
            small[taps + 2 : taps + 2 + nstate],
            small[taps + 2 + nstate :],
        )
        return (
            jnp.where(mine, own_gate, other_gate),
            parts,
            jnp.where(mine, x_proj[0], other_x),
            jnp.where(mine, dt_proj[0], other_dt),
        )

    inputs = lax.dynamic_index_in_dim(x_in, segment, 0, False)
    mixed_first = mixer(inputs, *weights(0))
    kept_first = lax.ppermute(mixed_first, "pipe", [(1, 0)])

    hidden = lax.dynamic_index_in_dim(hidden_in, segment, 0, False)
    hidden_parts = []
    for s in range(ctx):
        target = lax.rem(place + s, ctx)
        piece = lax.dynamic_slice_in_dim(hidden, target * depth, depth, 1)
        hidden_parts.append(piece if s == 0 else rotated(piece, "ctx", s))
    hidden_rows = jnp.stack(hidden_parts, axis=0)

    every = jnp.stack(
        [mixed_first] + [rotated(mixed_first, "ctx", s) for s in range(1, ctx)], axis=0
    ).reshape(ctx, tp, block, width)
    link = None
    for s in reversed(range(tp)):
        target = lax.rem(column + s, tp)
        rows = lax.dynamic_index_in_dim(every, target, 1, False).reshape(ctx * block, width)
        product = jnp.dot(rows, out_proj, preferred_element_type=F32)
        part = product if s == 0 else rotated(product.astype(BF16), "tp", s)
        link = part.astype(F32) if link is None else link + part.astype(F32)
    carried = (hidden_rows.reshape(ctx * block, depth).astype(F32) + link).astype(BF16)
    wide = carried.astype(F32)
    order = lax.rem(place - jnp.arange(ctx) + ctx, ctx)
    square = jnp.sum(wide * wide, axis=1).reshape(ctx, block)[order]
    squares = square
    for s in range(1, ctx):
        squares = squares + rotated(square, "ctx", s)
    scale = lax.rsqrt(squares[order].reshape(-1, 1) / (depth * ctx) + 1e-05)
    gain = lax.dynamic_slice_in_dim(norm_gain, place * depth, depth, 0)
    normed = (wide * scale * gain[None, :]).astype(BF16)

    products = []
    for s in range(tp):
        part = normed if s == 0 else rotated(normed, "tp", s)
        products.append(
            lax.dot_general(
                part, in_proj, (((1,), (1,)), ((), ())), preferred_element_type=F32
            ).reshape(ctx, block, width)
        )
    made = None
    for s in range(ctx):
        rows = jnp.stack([product[s] for product in products], axis=0)
        part = rows if s == 0 else rotated(rows.astype(BF16), "ctx", -s)
        made = part.astype(F32) if made is None else made + part.astype(F32)
    made = made.astype(BF16)
    inputs = jnp.concatenate(
        [
            lax.dynamic_index_in_dim(made, lax.rem(column - k + tp, tp), 0, False)
            for k in range(tp)
        ],
        axis=0,
    )
    mixed_second = mixer(inputs, *weights(1))
    kept_second = lax.ppermute(mixed_second, "pipe", [(0, 1)])
    low = jnp.where(first, mixed_first, kept_second)
    high = jnp.where(first, kept_first, mixed_second)
    return jnp.stack([low, high], axis=0)[None]


def solution(mesh):
    in_specs = (
        P(None, "ctx", "tp"),
        P(None, ("ctx", "tp"), None),
        P("pipe", None, "ctx", "tp"),
        P("tp", "ctx"),
        P("tp", "ctx"),
        P(),
        P("pipe", None, "tp"),
        P("pipe", "tp"),
        P("pipe", "tp", None),
        P("pipe", None, "tp"),
        P("pipe", "tp"),
        P("pipe", None, "tp"),
        P("pipe", "tp"),
    )
    out_specs = P("pipe", None, "ctx", "tp")
    return jax.shard_map(shards, mesh=mesh, in_specs=in_specs, out_specs=out_specs, check_vma=False)
```

```python
import functools

import jax
import jax.numpy as jnp
from jax import lax
from jax.experimental import pallas as pl
from jax.experimental.pallas import tpu as pltpu
from jax.sharding import PartitionSpec as P

LANES = 128
TILE = 1024
ROWS = 8
LOG2E = 1.4426950408889634
BF16 = jnp.bfloat16
F32 = jnp.float32


def params():
    return pltpu.CompilerParams(vmem_limit_bytes=32 * 1024 * 1024)


def rotated(block, axis, distance):
    count = lax.axis_size(axis)
    return lax.ppermute(block, axis, [(i, (i + distance) % count) for i in range(count)])


def shifted(block, axis, distance):
    count = lax.axis_size(axis)
    return lax.ppermute(block, axis, [(i - distance, i) for i in range(distance, count)])


def swapped(block):
    return lax.ppermute(block, "pipe", [(0, 1), (1, 0)])


def sibling(block):
    count = lax.axis_size("ctx")
    return lax.ppermute(block, "ctx", [(i, i ^ 1) for i in range(count)])


def swap_shared(weight):
    half = weight.shape[0] // 2
    core = lax.axis_index("ctx") % 2
    part = swapped(lax.dynamic_slice_in_dim(weight, core * half, half, 0))
    rest = sibling(part)
    first = core == 0
    return jnp.concatenate([jnp.where(first, part, rest), jnp.where(first, rest, part)], axis=0)


def conv_kernel(x_ref, rim_ref, w_ref, b_ref, proj_ref, act_ref, part_ref, pad, total):
    count, width = x_ref.shape
    taps = w_ref.shape[0]
    rim = rim_ref.shape[0]
    pad[:rim, :] = rim_ref[...].astype(F32)
    pad[rim:, :] = x_ref[...].astype(F32)
    for row in range(0, count, 32):
        value = b_ref[...] + jnp.zeros((32, width), F32)
        for k in range(taps):
            start = rim - (taps - 1) + row + k
            value = value + w_ref[k : k + 1, :] * pad[start : start + 32, :]
        act_ref[row : row + 32, :] = (value / (1.0 + jnp.exp(-value))).astype(BF16)
    product = jnp.dot(act_ref[...], proj_ref[...], preferred_element_type=F32)
    step = pl.program_id(0)

    @pl.when(step == 0)
    def _():
        total[...] = product

    @pl.when(step > 0)
    def _():
        total[...] += product

    @pl.when(step == pl.num_programs(0) - 1)
    def _():
        part_ref[...] = total[...].astype(BF16)


def conv_project(inputs, rim, conv_weight, conv_bias, x_proj):
    count, width = inputs.shape
    cols = x_proj.shape[1]
    block = 512
    return pl.pallas_call(
        conv_kernel,
        grid=(width // block,),
        in_specs=[
            pl.BlockSpec((count, block), lambda c: (0, c)),
            pl.BlockSpec((rim.shape[0], block), lambda c: (0, c)),
            pl.BlockSpec((conv_weight.shape[0], block), lambda c: (0, c)),
            pl.BlockSpec((1, block), lambda c: (0, c)),
            pl.BlockSpec((block, cols), lambda c: (c, 0)),
        ],
        out_specs=[
            pl.BlockSpec((count, block), lambda c: (0, c)),
            pl.BlockSpec((count, cols), lambda c: (0, 0)),
        ],
        out_shape=[
            jax.ShapeDtypeStruct((count, width), BF16),
            jax.ShapeDtypeStruct((count, cols), BF16),
        ],
        scratch_shapes=[
            pltpu.VMEM((count + rim.shape[0], block), F32),
            pltpu.VMEM((count, cols), F32),
        ],
        compiler_params=params(),
        name="conv_project",
    )(inputs, rim, conv_weight, conv_bias, x_proj)


def scan_kernel(nstate, maps_ref, rate_ref, dt_ref, bias_ref, act_ref, decay_ref,
                resp_ref, cum_ref, end_ref, steps, driven, wide):
    count = rate_ref.shape[0]
    wide[...] = jnp.dot(rate_ref[...], dt_ref[...], preferred_element_type=F32)

    def spread(group, carry):
        base = pl.multiple_of(group * 16, 16)
        for j in range(ROWS):
            lanes = slice(j * LANES, (j + 1) * LANES)
            raw = wide[pl.ds(base, 16), lanes] + bias_ref[:, lanes]
            rate = jnp.maximum(raw, 0.0) + jnp.log1p(jnp.exp(-jnp.abs(raw)))
            active = act_ref[pl.ds(base, 16), lanes].astype(F32)
            steps[pl.ds(base * ROWS + j, 16, stride=ROWS), :] = rate
            driven[pl.ds(base * ROWS + j, 16, stride=ROWS), :] = rate * active
        return carry

    lax.fori_loop(0, count // 16, spread, 0)

    def one(t, carry):
        state, cum = carry
        rows = pl.ds(pl.multiple_of(t * ROWS, ROWS), ROWS)
        rate = steps[rows, :]
        drive = driven[rows, :]
        later, sums = [], [None] * 4
        for n in range(nstate):
            h = jnp.exp2(rate * decay_ref[n]) * state[n] + maps_ref[t, n] * drive
            later.append(h)
            term = maps_ref[t, nstate + n] * h
            sums[n % 4] = term if sums[n % 4] is None else sums[n % 4] + term
        cum = cum + rate
        resp_ref[rows, :] = (sums[0] + sums[1]) + (sums[2] + sums[3])
        cum_ref[rows, :] = cum
        return tuple(later), cum

    def pair(g, carry):
        return one(2 * g + 1, one(2 * g, carry))

    zero = jnp.zeros((ROWS, LANES), F32)
    state, cum = lax.fori_loop(0, count // 2, pair, ((zero,) * nstate, zero))
    for n in range(nstate):
        end_ref[n] = state[n]
    end_ref[nstate] = cum


def local_scan(maps, rate_normed, dt_proj, dt_bias, activated, decay):
    count, width = activated.shape
    rank = dt_proj.shape[0]
    nstate = decay.shape[0]
    tiles = width // TILE
    rows = pl.BlockSpec((None, count * ROWS, LANES), lambda c: (c, 0, 0))
    return pl.pallas_call(
        functools.partial(scan_kernel, nstate),
        grid=(tiles,),
        in_specs=[
            pl.BlockSpec(memory_space=pltpu.SMEM),
            pl.BlockSpec((count, rank), lambda c: (0, 0)),
            pl.BlockSpec((rank, TILE), lambda c: (0, c)),
            pl.BlockSpec((1, TILE), lambda c: (0, c)),
            pl.BlockSpec((count, TILE), lambda c: (0, c)),
            pl.BlockSpec((nstate, ROWS, LANES), lambda c: (0, c, 0)),
        ],
        out_specs=[rows, rows, pl.BlockSpec((nstate + 1, ROWS, LANES), lambda c: (0, c, 0))],
        out_shape=[
            jax.ShapeDtypeStruct((tiles, count * ROWS, LANES), F32),
            jax.ShapeDtypeStruct((tiles, count * ROWS, LANES), F32),
            jax.ShapeDtypeStruct((nstate + 1, tiles * ROWS, LANES), F32),
        ],
        scratch_shapes=[
            pltpu.VMEM((count * ROWS, LANES), F32),
            pltpu.VMEM((count * ROWS, LANES), F32),
            pltpu.VMEM((count, TILE), F32),
        ],
        compiler_params=params(),
        name="local_scan",
    )(maps, rate_normed, dt_proj, dt_bias, activated, decay)


def finish_kernel(nstate, earlier, maps_ref, resp_ref, cum_ref, decay_ref, skip_ref,
                  act_ref, gate_ref, *rest):
    ends, out_ref, total, enter = rest[:earlier], rest[earlier], rest[earlier + 1], rest[earlier + 2]
    count = act_ref.shape[0]
    for n in range(nstate):
        value, passed = ends[0][n], ends[0][nstate]
        for block in ends[1:]:
            value = value + jnp.exp2(decay_ref[n] * passed) * block[n]
            passed = passed + block[nstate]
        enter[n] = value

    def one(t):
        rows = pl.ds(pl.multiple_of(t * ROWS, ROWS), ROWS)
        cum = cum_ref[rows, :]
        sums = [resp_ref[rows, :], None, None, None]
        for n in range(nstate):
            term = maps_ref[t, nstate + n] * (jnp.exp2(cum * decay_ref[n]) * enter[n])
            sums[n % 4] = term if sums[n % 4] is None else sums[n % 4] + term
        total[rows, :] = (sums[0] + sums[1]) + (sums[2] + sums[3])

    def pair(g, carry):
        one(2 * g)
        one(2 * g + 1)
        return carry

    lax.fori_loop(0, count // 2, pair, 0)

    def gather(group, carry):
        base = pl.multiple_of(group * 16, 16)
        for j in range(ROWS):
            lanes = slice(j * LANES, (j + 1) * LANES)
            active = act_ref[pl.ds(base, 16), lanes].astype(F32)
            gate = gate_ref[pl.ds(base, 16), lanes].astype(F32)
            value = total[pl.ds(base * ROWS + j, 16, stride=ROWS), :] + skip_ref[:, lanes] * active
            out_ref[pl.ds(base, 16), lanes] = (value * (gate / (1.0 + jnp.exp(-gate)))).astype(BF16)
        return carry

    lax.fori_loop(0, count // 16, gather, 0)


def finish(maps, response, cum, decay, skip, activated, gate, ends):
    count, width = activated.shape
    nstate = decay.shape[0]
    rows = pl.BlockSpec((None, count * ROWS, LANES), lambda c: (c, 0, 0))
    flat = pl.BlockSpec((count, TILE), lambda c: (0, c))
    return pl.pallas_call(
        functools.partial(finish_kernel, nstate, len(ends)),
        grid=(width // TILE,),
        in_specs=[
            pl.BlockSpec(memory_space=pltpu.SMEM),
            rows,
            rows,
            pl.BlockSpec((nstate, ROWS, LANES), lambda c: (0, c, 0)),
            pl.BlockSpec((1, TILE), lambda c: (0, c)),
            flat,
            flat,
        ]
        + [pl.BlockSpec((nstate + 1, ROWS, LANES), lambda c: (0, c, 0))] * len(ends),
        out_specs=flat,
        out_shape=jax.ShapeDtypeStruct((count, width), BF16),
        scratch_shapes=[
            pltpu.VMEM((count * ROWS, LANES), F32),
            pltpu.VMEM((nstate, ROWS, LANES), F32),
        ],
        compiler_params=params(),
        name="finish_mixer",
    )(maps, response, cum, decay, skip, activated, gate, *ends)


def mixer(inputs, gate, small, x_proj, dt_proj):
    conv_weight, conv_bias, dt_bias, decay, skip = small
    rank = dt_proj.shape[0]
    nstate = decay.shape[0]
    rim = shifted(inputs[-16:], "ctx", 1)
    activated, partial = conv_project(inputs, rim, conv_weight, conv_bias, x_proj)
    parts = [partial] + [rotated(partial, "tp", s) for s in range(1, lax.axis_size("tp"))]
    projected = parts[0].astype(F32)
    for part in parts[1:]:
        projected = projected + part.astype(F32)
    low = projected[:, :rank]
    rate_normed = (
        low * lax.rsqrt(jnp.mean(low * low, axis=1, keepdims=True) + 1e-06)
    ).astype(BF16)
    maps = projected[:, rank:]
    decay_tiles = (decay * -LOG2E).reshape(nstate, -1, LANES)
    response, cum, end = local_scan(maps, rate_normed, dt_proj, dt_bias, activated, decay_tiles)
    ends = [shifted(end, "ctx", s) for s in range(1, lax.axis_size("ctx"))]
    return finish(maps, response, cum, decay_tiles, skip, activated, gate, ends)


def shards(
    x_in,
    hidden_in,
    gate_z,
    out_proj,
    in_proj,
    norm_gain,
    conv_weight,
    conv_bias,
    x_proj,
    dt_proj,
    dt_bias,
    decay_rate,
    skip,
):
    segment = lax.axis_index("pipe")
    first = segment == 0
    ctx, tp = lax.axis_size("ctx"), lax.axis_size("tp")
    place, column = lax.axis_index("ctx"), lax.axis_index("tp")
    block = hidden_in.shape[1]
    depth = out_proj.shape[1]
    width = x_in.shape[2]

    own_small = jnp.concatenate(
        [conv_weight[0], conv_bias, dt_bias, decay_rate[0], skip], axis=0
    )
    other_small = swapped(own_small)
    other_x = swap_shared(x_proj[0])
    held_dt, other_x = lax.optimization_barrier((dt_proj[0], other_x))
    other_dt = swap_shared(held_dt)
    own_gate = lax.dynamic_index_in_dim(gate_z[0], segment, 0, False)
    held_gate, other_dt = lax.optimization_barrier(
        (lax.dynamic_index_in_dim(gate_z[0], 1 - segment, 0, False), other_dt)
    )
    other_gate = swapped(held_gate)
    taps = conv_weight.shape[1]
    nstate = decay_rate.shape[1]

    def weights(section):
        mine = first if section == 0 else jnp.logical_not(first)
        small = jnp.where(mine, own_small, other_small)
        parts = (
            small[:taps],
            small[taps : taps + 1],
            small[taps + 1 : taps + 2],
            small[taps + 2 : taps + 2 + nstate],
            small[taps + 2 + nstate :],
        )
        return (
            jnp.where(mine, own_gate, other_gate),
            parts,
            jnp.where(mine, x_proj[0], other_x),
            jnp.where(mine, dt_proj[0], other_dt),
        )

    inputs = lax.dynamic_index_in_dim(x_in, segment, 0, False)
    mixed_first = mixer(inputs, *weights(0))
    kept_first = lax.ppermute(mixed_first, "pipe", [(1, 0)])

    hidden = lax.dynamic_index_in_dim(hidden_in, segment, 0, False)
    hidden_parts = []
    for s in range(0, ctx, 2):
        target = lax.rem(place + s, ctx)
        piece = lax.dynamic_slice_in_dim(hidden, target * depth, depth, 1)
        hidden_parts.append(piece if s == 0 else rotated(piece, "ctx", s))
        piece = lax.dynamic_slice_in_dim(hidden, (target ^ 1) * depth, depth, 1)
        route = [(i, ((i + s) % ctx) ^ 1) for i in range(ctx)]
        hidden_parts.append(lax.ppermute(piece, "ctx", route))
    hidden_rows = jnp.stack(hidden_parts, axis=0)

    fetched = []
    for s in range(0, ctx, 2):
        part = mixed_first if s == 0 else rotated(mixed_first, "ctx", s)
        fetched += [part, sibling(part)]
    every = jnp.stack(fetched, axis=0).reshape(ctx, tp, block, width)
    link = None
    for s in reversed(range(tp)):
        target = lax.rem(column + s, tp)
        rows = lax.dynamic_index_in_dim(every, target, 1, False).reshape(ctx * block, width)
        product = jnp.dot(rows, out_proj, preferred_element_type=F32)
        part = product if s == 0 else rotated(product.astype(BF16), "tp", s)
        link = part.astype(F32) if link is None else link + part.astype(F32)
    carried = (hidden_rows.reshape(ctx * block, depth).astype(F32) + link).astype(BF16)
    wide = carried.astype(F32)
    index = jnp.arange(ctx)
    odd = index % 2
    holder = lax.rem((place ^ odd) - (index - odd) + ctx, ctx)
    apart = (index ^ place) & 1
    slot = lax.rem((place ^ apart) - index + ctx, ctx) + apart
    square = jnp.sum(wide * wide, axis=1).reshape(ctx, block)[slot]
    squares = square
    for s in range(1, ctx):
        squares = squares + rotated(square, "ctx", s)
    scale = lax.rsqrt(squares[holder].reshape(-1, 1) / (depth * ctx) + 1e-05)
    gain = lax.dynamic_slice_in_dim(norm_gain, place * depth, depth, 0)
    normed = (wide * scale * gain[None, :]).astype(BF16)

    products = []
    for s in range(tp):
        part = normed if s == 0 else rotated(normed, "tp", s)
        products.append(
            lax.dot_general(
                part, in_proj, (((1,), (1,)), ((), ())), preferred_element_type=F32
            ).reshape(ctx, block, width)
        )
    made = None
    for s in reversed(range(0, ctx, 2)):
        rows = jnp.stack([product[s] for product in products], axis=0)
        others = jnp.stack([product[s + 1] for product in products], axis=0)
        rows = rows + sibling(others.astype(BF16)).astype(F32)
        part = rows if s == 0 else rotated(rows.astype(BF16), "ctx", -s)
        made = part.astype(F32) if made is None else made + part.astype(F32)
    made = made.astype(BF16)
    inputs = jnp.concatenate(
        [
            lax.dynamic_index_in_dim(made, lax.rem(column - k + tp, tp), 0, False)
            for k in range(tp)
        ],
        axis=0,
    )
    mixed_second = mixer(inputs, *weights(1))
    kept_second = lax.ppermute(mixed_second, "pipe", [(0, 1)])
    low = jnp.where(first, mixed_first, kept_second)
    high = jnp.where(first, kept_first, mixed_second)
    return jnp.stack([low, high], axis=0)[None]


def solution(mesh):
    in_specs = (
        P(None, "ctx", "tp"),
        P(None, ("ctx", "tp"), None),
        P("pipe", None, "ctx", "tp"),
        P("tp", "ctx"),
        P("tp", "ctx"),
        P(),
        P("pipe", None, "tp"),
        P("pipe", "tp"),
        P("pipe", "tp", None),
        P("pipe", None, "tp"),
        P("pipe", "tp"),
        P("pipe", None, "tp"),
        P("pipe", "tp"),
    )
    out_specs = P("pipe", None, "ctx", "tp")
    return jax.shard_map(shards, mesh=mesh, in_specs=in_specs, out_specs=out_specs, check_vma=False)
```
